32 devices in a mesh: dp: 4 (over y, x), fsdp: 8 (over z, core).
Axes of the slice: x: 2, y: 2, z: 4, core: 2. Of those that a mesh axis runs over, the one named last changes fastest.
Arguments:
- tokens: bfloat16 [32, 1024, 512], P(('dp', 'fsdp')), may hold values from -6 to 6
- lengths: int32 [32], P(('dp', 'fsdp')), may hold values from 128 to 1024, as said below
- routes: int32 [32, 1024, 8], P(('dp', 'fsdp')), may hold values from 0 to 23, all different within a row
- query_weight: bfloat16 [512, 1536], P(('dp', 'fsdp')), may hold values from -0.25 to 0.25
- key_value_weight: bfloat16 [512, 128], P(('dp', 'fsdp')), may hold values from -0.25 to 0.25
- router_weight: bfloat16 [512, 24], P(('dp', 'fsdp')), may hold values from -0.125 to 0.125
- output_weight: bfloat16 [1536, 512], P(('dp', 'fsdp')), may hold values from -16 to 16
- expand_weight: bfloat16 [512, 2048], P(('dp', 'fsdp')), may hold values from -0.25 to 0.25
- expand_bias: bfloat16 [2048], P(('dp', 'fsdp')), may hold values from -3 to 3
- reduce_weight: bfloat16 [2048, 512], P(('dp', 'fsdp')), may hold values from -0.1875 to 0.1875
- reduce_bias: bfloat16 [512], P(('dp', 'fsdp')), may hold values from -1.75 to 1.75
- first_gain: bfloat16 [512], P(('dp', 'fsdp')), may hold values from 0.25 to 1.75
- first_bias: bfloat16 [512], P(('dp', 'fsdp')), may hold values from -1.75 to 1.75
- second_gain: bfloat16 [512], P(('dp', 'fsdp')), may hold values from 0.25 to 1.75
- second_bias: bfloat16 [512], P(('dp', 'fsdp')), may hold values from -1.75 to 1.75
- cotangent: bfloat16 [32, 1024, 512], P(('dp', 'fsdp')), may hold values from -6 to 6
Outputs:
- output: bfloat16 [32, 1024, 512], P(('dp', 'fsdp'))
- tokens_grad: bfloat16 [32, 1024, 512], P(('dp', 'fsdp'))
- query_weight_grad: float32 [512, 1536], P(('dp', 'fsdp'))
- key_value_weight_grad: float32 [512, 128], P(('dp', 'fsdp'))
- router_weight_grad: float32 [512, 24], P(('dp', 'fsdp'))
- output_weight_grad: float32 [1536, 512], P(('dp', 'fsdp'))
- expand_weight_grad: float32 [512, 2048], P(('dp', 'fsdp'))
- expand_bias_grad: float32 [2048], P(('dp', 'fsdp'))
- reduce_weight_grad: float32 [2048, 512], P(('dp', 'fsdp'))
- reduce_bias_grad: float32 [512], P(('dp', 'fsdp'))
- first_gain_grad: float32 [512], P(('dp', 'fsdp'))
- first_bias_grad: float32 [512], P(('dp', 'fsdp'))
- second_gain_grad: float32 [512], P(('dp', 'fsdp'))
- second_bias_grad: float32 [512], P(('dp', 'fsdp'))
- router_stats: float32 [2, 24], replicated
The draws below stay inside these ranges and needn't reach their ends.
Inputs may be any that keep to these rules, and one draw needn't show every extreme that they name: Sequence s holds valid tokens at slots below lengths[s], padding after them; some sequence has exactly 1024. `routes`: each token names 8 different head experts.
All inputs are finite; a program needn't handle non-finite values.
Results may differ from the reference program's by a relative error of at most 0.012.
Values may be sent and summed in bfloat16 or wider, within the bound.
No kernel may reach another device: no remote copies, remote signals or barrier semaphores. Data moves between devices by JAX's collectives and lax.ppermute only.
A program may use at most 128 MiB of HBM per device.

```python
import jax
import jax.numpy as jnp
from jax import lax

D = 512
HD = 64
E = 24
TOPK = 8
FF = 2048
LEN = 1024
SEQS = 32


def draw_lengths(key, part):
    key = jax.random.fold_in(key, 11)
    draw_key, pick_key = jax.random.split(key)
    values = jax.random.randint(draw_key, (SEQS,), LEN // 8, LEN + 1)
    chosen = jax.random.randint(pick_key, (), 0, SEQS)
    return jnp.where(jnp.arange(SEQS) == chosen, LEN, values).astype(jnp.int32)


def block_levels(key, shape, cuts, smallest, high):
    level = 1.0
    for position, blocks in cuts:
        steps = jax.random.uniform(jax.random.fold_in(jax.random.fold_in(key, 6), position), (blocks,), jnp.float32, smallest / len(cuts), high / len(cuts))
        level = level * jnp.repeat(jnp.exp(steps), shape[position] // blocks).reshape((-1,) + (1,) * (len(shape) - 1 - position))
    return level


def different_ones(rng, rows, amount, top, lift):
    order = jax.random.permutation(jax.random.fold_in(rng, 1), amount)
    boost = order
    for power in range(3):
        boost = boost * boost // amount
    boost = boost * lift // amount
    lots = jax.random.randint(jax.random.fold_in(rng, 2), (rows, amount), 0, 4096) + boost
    sure = jax.random.permutation(jax.random.fold_in(rng, 3), rows)[jnp.arange(amount) % rows]
    lots = jnp.where(jnp.arange(rows)[:, None] == sure[None, :], 1 << 14, lots)
    merit = lots * amount + jnp.arange(amount)
    return lax.top_k(merit.astype(jnp.int32), top)[1].astype(jnp.int32)


def gaussian(own_key, shape, scale, limit, cuts=(), held_as=jnp.bfloat16):
    drawn = scale * jax.random.normal(own_key, shape, jnp.float32)
    if cuts:
        drawn = drawn * block_levels(own_key, shape, cuts, -0.22, 0.18)
    return jnp.clip(drawn, -limit, limit).astype(held_as)


def setup_inputs(seed: int = 0) -> dict:
    key_list = jax.random.split(jax.random.key(seed), 17)
    return {
        "tokens": gaussian(key_list[0], (SEQS, LEN, D), 1.0, 6.0, ((0, 32),)),
        "lengths": draw_lengths(jax.random.fold_in(key_list[16], 71), 0),
        "routes": different_ones(key_list[2], SEQS * LEN, E, TOPK, 2730).reshape((SEQS, LEN, TOPK)),
        "query_weight": gaussian(key_list[3], (D, E * HD), D ** -0.5, 0.25, ((0, 32),)),
        "key_value_weight": gaussian(key_list[4], (D, 2 * HD), D ** -0.5, 0.25, ((0, 32),)),
        "router_weight": gaussian(key_list[5], (D, E), (4 * D) ** -0.5, 0.125, ((0, 32),)),
        "output_weight": gaussian(key_list[6], (E * HD, D), 3.0, 16.0, ((0, 32),)),
        "expand_weight": gaussian(key_list[7], (D, FF), D ** -0.5, 0.25, ((0, 32),)),
        "expand_bias": gaussian(key_list[8], (FF,), 0.5, 3.0, ((0, 32),)),
        "reduce_weight": gaussian(key_list[9], (FF, D), (FF // 2) ** -0.5, 0.1875, ((0, 32),)),
        "reduce_bias": gaussian(key_list[10], (D,), 0.3, 1.75, ((0, 32),)),
        "first_gain": jnp.clip(1.0 + 0.15 * jax.random.normal(key_list[11], (D,), jnp.float32), 0.25, 1.75).astype(jnp.bfloat16),
        "first_bias": gaussian(key_list[12], (D,), 0.3, 1.75, ((0, 32),)),
        "second_gain": jnp.clip(1.0 + 0.15 * jax.random.normal(key_list[13], (D,), jnp.float32), 0.25, 1.75).astype(jnp.bfloat16),
        "second_bias": gaussian(key_list[14], (D,), 0.3, 1.75, ((0, 32),)),
        "cotangent": gaussian(key_list[15], (SEQS, LEN, D), 1.0, 6.0, ((0, 32),)),
    }


HIGHEST = lax.Precision.HIGHEST

@jax.custom_vjp
def low(v):
    return lax.optimization_barrier(v.astype(jnp.bfloat16)).astype(jnp.float32)

@jax.custom_vjp
def low_back(v):
    return v

def low_keep(v):
    return (low(v), None)

def low_pass(kept, grad):
    return (grad,)

def back_keep(v):
    return (v, None)

def back_low(kept, grad):
    return (low(grad),)
low.defvjp(low_keep, low_pass)
low_back.defvjp(back_keep, back_low)

def matmul(left, right):
    return jnp.dot(left, right, precision=HIGHEST, preferred_element_type=jnp.float32)

def layer_norm(values, norm_gain, norm_bias):
    center = values - lax.optimization_barrier(jnp.mean(values, axis=-1, keepdims=True))
    spread = lax.optimization_barrier(jnp.mean(center * center, axis=-1, keepdims=True))
    return center * lax.rsqrt(spread + 1e-05) * norm_gain + norm_bias

def block_forward(sequence, length, route_rows, params):
    query_weight, key_value_weight, router_weight, output_weight, expand_weight, expand_bias, reduce_weight, reduce_bias, first_gain, first_bias, second_gain, second_bias = params
    normed = low(layer_norm(sequence, first_gain, first_bias))
    onehot = (route_rows[:, :, None] == jnp.arange(E)[None, None, :]).astype(jnp.float32)
    query_all = matmul(normed, query_weight).reshape(LEN, E, HD)
    queries = low_back(low(jnp.einsum('tje,ted->tjd', onehot, query_all, precision=HIGHEST)))
    key_value = low_back(low(matmul(normed, key_value_weight)))
    key_rows = key_value[:, :HD]
    value_rows = key_value[:, HD:]
    logits = low_back(matmul(normed, router_weight))
    picked = jnp.einsum('tje,te->tj', onehot, logits, precision=HIGHEST)
    gating = jax.nn.softmax(picked, axis=-1)
    router_probs = jax.nn.softmax(logits, axis=-1)
    scores = low_back(jnp.einsum('tjd,sd->tjs', queries, key_rows, precision=HIGHEST) * HD ** (-0.5))
    places = jnp.arange(LEN)
    allowed = (places[None, :] <= places[:, None]) & (places[None, :] < length)
    scores = jnp.where(allowed[:, None, :], scores, -1e+30)
    weights_soft = low(jax.nn.softmax(scores, axis=-1))
    mixed_out = low_back(jnp.einsum('tjs,sd->tjd', weights_soft, value_rows, precision=HIGHEST))
    spread_out = low(jnp.einsum('tje,tj,tjd->ted', onehot, gating, mixed_out, precision=HIGHEST)).reshape(LEN, E * HD)
    attended = low_back(matmul(spread_out, output_weight))
    middle = sequence + attended
    normed_two = low(layer_norm(middle, second_gain, second_bias))
    expanded = low_back(matmul(normed_two, expand_weight) + expand_bias)
    activated = low(jax.nn.gelu(expanded))
    reduced = low_back(matmul(activated, reduce_weight) + reduce_bias)
    result = middle + reduced
    valid_rows = (places < length).astype(jnp.float32)
    return (result, lax.optimization_barrier(jnp.sum(router_probs * valid_rows[:, None], axis=0)))

def reference(tokens, lengths, routes, query_weight, key_value_weight, router_weight, output_weight, expand_weight, expand_bias, reduce_weight, reduce_bias, first_gain, first_bias, second_gain, second_bias, cotangent):
    params = (query_weight.astype(jnp.float32), key_value_weight.astype(jnp.float32), router_weight.astype(jnp.float32), output_weight.astype(jnp.float32), expand_weight.astype(jnp.float32), expand_bias.astype(jnp.float32), reduce_weight.astype(jnp.float32), reduce_bias.astype(jnp.float32), first_gain.astype(jnp.float32), first_bias.astype(jnp.float32), second_gain.astype(jnp.float32), second_bias.astype(jnp.float32))
    inputs = tokens.astype(jnp.float32)

    def whole_layer(layer_inputs, layer_params):

        def one_sequence(seq_item):
            return jax.checkpoint(block_forward)(seq_item[0], seq_item[1], seq_item[2], layer_params)
        result, sums = lax.map(one_sequence, (layer_inputs, lengths, routes))
        return (result, lax.optimization_barrier(jnp.sum(sums, axis=0)))
    result, pullback, prob_sums = jax.vjp(whole_layer, inputs, params, has_aux=True)
    input_grad, param_grads = pullback(cotangent.astype(jnp.float32))
    valid_rows = (jnp.arange(LEN)[None, :] < lengths[:, None]).astype(jnp.float32)
    matches = (routes[:, :, :, None] == jnp.arange(E)[None, None, None, :]).astype(jnp.float32)
    counts = lax.optimization_barrier(jnp.sum(valid_rows[:, :, None, None] * matches, axis=(0, 1, 2)))
    valid_total = jnp.sum(valid_rows)
    router_stats = jnp.stack([E * counts / (TOPK * valid_total), E * prob_sums / valid_total])
    return (result.astype(jnp.bfloat16), input_grad.astype(jnp.bfloat16), param_grads[0], param_grads[1], param_grads[2], param_grads[3], param_grads[4], param_grads[5], param_grads[6], param_grads[7], param_grads[8], param_grads[9], param_grads[10], param_grads[11], router_stats)
```

```python
import functools
import math

import jax
import jax.numpy as jnp
from jax import lax
from jax.experimental import pallas as pl
from jax.experimental.pallas import tpu as pltpu
from jax.sharding import PartitionSpec as P

D = 512
HD = 64
E = 24
TOPK = 8
FF = 2048
T = 1024
NB = 32
QW = E * HD
C1 = QW + 256
MISC = QW + 128
C2 = 3 * 512 + FF + 4 * 512
VG = E
ST = 40
SCALE2 = HD**-0.5 * math.log2(math.e)
NEG = -1e30
BF = jnp.bfloat16
F32 = jnp.float32
AXES = ("dp", "fsdp")


def nt(a, b):
    return lax.dot_general(a, b, (((1,), (1,)), ((), ())), preferred_element_type=F32)


def nn(a, b):
    return lax.dot_general(a, b, (((1,), (0,)), ((), ())), preferred_element_type=F32)


def rows_at(i, n):
    return pl.ds(pl.multiple_of(i * n, n), n)


def fold8(x, op):
    return op(x.reshape(x.shape[0] // 8, 8, x.shape[1]), axis=0)


def select_slots(src, routes, lanes, dst_store):
    for half in range(2):
        r = [jnp.broadcast_to(routes[j : j + 1, :], (32, lanes)) for j in range(TOPK)]
        acc = [jnp.zeros((32, lanes), F32) for _ in range(TOPK)]
        for e in range(E):
            block = src(e * HD + half * 32)
            for j in range(TOPK):
                acc[j] = jnp.where(r[j] == e, block, acc[j])
        for j in range(TOPK):
            dst_store(j, half, acc[j])


def spread_slots(vals, routes, lanes, dst_store):
    for half in range(2):
        r = [jnp.broadcast_to(routes[j : j + 1, :], (32, lanes)) for j in range(TOPK)]
        v = [vals(j, half) for j in range(TOPK)]
        for e in range(E):
            acc = jnp.zeros((32, lanes), F32)
            for j in range(TOPK):
                acc = jnp.where(r[j] == e, v[j], acc)
            dst_store(e, half, acc.astype(BF))


def split_terms(x, n):
    terms = []
    for _ in range(n):
        t = x.astype(BF).astype(F32)
        terms.append(t)
        x = x - t
    return terms


def project_kernel(n_pieces, dst, length, tok, rt, *refs):
    pieces = refs[:n_pieces]
    (w1, normed_t, q_t, kv_t, ka, va, gate_t, misc, stat, ebias, w1_t, qa, psum, csum, eb) = refs[n_pieces:]
    at = 0
    for piece in pieces:
        for r in range(piece.shape[0]):
            w1[rows_at(dst[at + r], 16), :] = piece[r]
        at += piece.shape[0]
    for c in range(C1 // 128):
        w1_t[128 * c : 128 * (c + 1), :] = w1[:, 128 * c : 128 * (c + 1)].T
    misc[...] = w1_t[MISC:, :].astype(F32)
    lanes = lax.broadcasted_iota(jnp.int32, (16, 128), 1)
    for i in range(NB):
        tail = w1[16 * i : 16 * (i + 1), MISC:].astype(F32)
        for c in range(4):
            column = jnp.sum(jnp.where(lanes == VG + 5 + c, tail, 0.0), axis=1, keepdims=True)
            eb[64 * i + 16 * c : 64 * i + 16 * (c + 1), :] = jnp.broadcast_to(column, (16, 128))
    ebias[...] = eb[...].T[:8, :]
    gain, bias = misc[VG : VG + 1, :], misc[VG + 1 : VG + 2, :]
    psum[...] = jnp.zeros_like(psum)
    csum[...] = jnp.zeros_like(csum)
    n_valid = length[0]

    def block(b, carry):
        cols = rows_at(b, 256)
        x = tok[cols, :].astype(F32)
        center = x - jnp.mean(x, axis=-1, keepdims=True)
        var = jnp.mean(center * center, axis=-1, keepdims=True)
        normed = (center * lax.rsqrt(var + 1e-05) * gain + bias).astype(BF)
        n_t = normed.T
        normed_t[:, cols] = n_t
        qa[...] = nn(w1_t[...], n_t)
        kv_t[:, cols] = qa[QW : QW + 128, :].astype(BF)
        logits = qa[MISC : MISC + E, :]
        routes = rt[:, cols]
        for h in range(2):
            lane = slice(128 * h, 128 * h + 128)

            def store(j, half, acc, h=h):
                q_t[64 * j + 32 * half : 64 * j + 32 * half + 32, rows_at(2 * b + h, 128)] = acc.astype(BF)

            select_slots(
                lambda row, lane=lane: qa[row : row + 32, lane], routes[:, lane], 128, store
            )
        ids = lax.broadcasted_iota(jnp.int32, (E, 256), 0)
        valid = (lax.broadcasted_iota(jnp.int32, (1, 256), 1) + b * 256 < n_valid).astype(F32)
        picked = []
        hits = jnp.zeros((E, 256), F32)
        for j in range(TOPK):
            hit = ids == jnp.broadcast_to(routes[j : j + 1, :], (E, 256))
            picked.append(jnp.sum(jnp.where(hit, logits, 0.0), axis=0, keepdims=True))
            hits = hits + jnp.where(hit, 1.0, 0.0)
        picked = jnp.concatenate(picked, axis=0)
        expo = jnp.exp(picked - jnp.max(picked, axis=0, keepdims=True))
        gate_t[:, cols] = expo / jnp.sum(expo, axis=0, keepdims=True)
        expo = jnp.exp(logits - jnp.max(logits, axis=0, keepdims=True))
        probs = expo / jnp.sum(expo, axis=0, keepdims=True) * valid
        hits = hits * valid
        psum[...] += probs[:, :128] + probs[:, 128:]
        csum[...] += hits[:, :128] + hits[:, 128:]
        return carry

    lax.fori_loop(0, T // 256, block, 0)
    lane = lax.broadcasted_iota(jnp.int32, (T, 64), 1)
    slot = lax.broadcasted_iota(jnp.int32, (T, 64), 0)
    kv = kv_t[...].T
    mask = jnp.where(slot < n_valid, 0.0, NEG)
    ka[:, :64] = kv[:, :64]
    ka[:, 64:] = jnp.where(lane == 0, mask, jnp.where(lane < 4, 1.0, 0.0)).astype(BF)
    va[:, :64] = kv[:, 64:]
    va[:, 64:] = jnp.where(lane < 2, 1.0, 0.0).astype(BF)
    counts = jnp.sum(csum[...], axis=1, keepdims=True)
    probs = jnp.floor(jnp.sum(psum[...], axis=1, keepdims=True) * 128.0 + 0.5)
    lanes = lax.broadcasted_iota(jnp.int32, (E, 128), 1)
    tile = jnp.zeros((E, 128), F32)
    for value, first, digits in ((counts, 0, 4), (probs, 4, 6)):
        for k in range(digits):
            rest = jnp.floor(value * 0.125)
            tile = jnp.where(lanes == ST + first + k, value - 8.0 * rest, tile)
            value = rest
    low = jnp.concatenate([tile[16:, :], jnp.zeros((8, 128), F32)], axis=0)
    stat[...] = tile[:16, :] + pltpu.roll(low, 10, axis=1)


def attend_kernel(lo, hi, q_t, ka, kv_t, gate_t, rt, mix_t, lse, sp_t, q_s, s_s, acc_s):
    row = lax.broadcasted_iota(jnp.int32, (64, 1024), 0)
    q_s[64:, :] = jnp.where(row == 0, 1.0, 0.0).astype(BF)

    def block(b, carry):
        cols = rows_at(b, 128)
        own = rows_at(b - lo, 128)
        for j in range(TOPK):
            q_s[:64, 128 * j : 128 * (j + 1)] = q_t[64 * j : 64 * (j + 1), cols]
        full = b // 2

        def scores(c, m):
            s = nn(ka[rows_at(c, 256), :], q_s[...])
            s_s[rows_at(c, 256), :] = s
            return jnp.maximum(m, fold8(s, jnp.max))

        m = lax.fori_loop(0, full, scores, jnp.full((8, 1024), NEG, F32))
        s = nn(ka[rows_at(full, 256), :], q_s[...])
        at_s = lax.broadcasted_iota(jnp.int32, (256, 1024), 0) + full * 256
        at_t = (lax.broadcasted_iota(jnp.int32, (256, 1024), 1) & 127) + b * 128
        s = jnp.where(at_s <= at_t, s, NEG)
        s_s[rows_at(full, 256), :] = s
        m = jnp.max(jnp.maximum(m, fold8(s, jnp.max)), axis=0, keepdims=True)
        acc_s[...] = jnp.zeros_like(acc_s)

        def values(c, total):
            e = jnp.exp2((s_s[rows_at(c, 256), :] - m) * SCALE2)
            acc_s[...] += nn(kv_t[64:, rows_at(c, 256)], e.astype(BF))
            return total + fold8(e, jnp.sum)

        total = lax.fori_loop(0, full + 1, values, jnp.zeros((8, 1024), F32))
        total = jnp.sum(total, axis=0, keepdims=True)
        top = m + jnp.log(total) * HD**0.5
        inv = 1.0 / total
        for j in range(TOPK):
            lane = slice(128 * j, 128 * (j + 1))
            lse[j : j + 1, own] = top[:, lane]
            mix_t[64 * j : 64 * (j + 1), own] = acc_s[:, lane] * inv[:, lane]
        gate = gate_t[:, cols]

        def vals(j, half):
            at = 64 * j + 32 * half
            return mix_t[at : at + 32, own] * gate[j : j + 1, :]

        def store(e, half, block):
            at = 64 * e + 32 * half
            sp_t[at : at + 32, own] = block

        spread_slots(vals, rt[:, cols], 128, store)
        return carry

    lax.fori_loop(lo, hi, block, 0)


def join(parts, whole):
    at = 0
    for part in parts:
        whole[:, at : at + part.shape[1]] = part[...]
        at += part.shape[1]


def ffn_kernel(n_pieces, n_parts, dst, tok, cot, vec, ebias, *refs):
    pieces, parts = refs[:n_pieces], refs[n_pieces : n_pieces + n_parts]
    (out, middle, dexp, wo, we, sp_t, sends, keeps, rsum, ebg, wr, act, n2_t, grad) = refs[
        n_pieces + n_parts :
    ]
    join(parts, sp_t)
    at = 0
    for piece in pieces:
        for r in range(piece.shape[0]):
            i = dst[at + r]
            for q in range(3):
                wo[rows_at(3 * i + q, 16), :] = piece[r, :, 512 * q : 512 * (q + 1)]
            we[rows_at(i, 16), :] = piece[r, :, 1536 : 1536 + FF]
            for q in range(4):
                wr[rows_at(4 * i + q, 16), :] = piece[
                    r, :, 1536 + FF + 512 * q : 1536 + FF + 512 * (q + 1)
                ]
        at += piece.shape[0]
    gain, bias = vec[VG + 2 : VG + 3, :], vec[VG + 3 : VG + 4, :]
    rbias = vec[VG + 4 : VG + 5, :]
    ebg[...] = jnp.zeros_like(ebg)
    rsum[...] = jnp.zeros_like(rsum)
    c0, c1 = math.sqrt(2.0 / math.pi), 0.044715

    def block(b, carry):
        rows = rows_at(b, 256)
        mid = tok[rows, :].astype(F32) + nn(sp_t[:, rows].T, wo[...])
        middle[rows, :] = mid
        center = mid - jnp.mean(mid, axis=-1, keepdims=True)
        var = jnp.mean(center * center, axis=-1, keepdims=True)
        n2 = (center * lax.rsqrt(var + 1e-05) * gain + bias).astype(BF)
        n2_t[:, rows] = n2.T
        dy = cot[rows, :]
        red = jnp.zeros((256, 512), F32)
        for f in range(FF // 512):
            fs = slice(512 * f, 512 * (f + 1))
            u = nn(n2, we[:, fs]) + ebias[0:1, fs]
            da = nt(dy, wr[fs, :])
            sq = u * u
            th = jnp.tanh(c0 * u * (1.0 + c1 * sq))
            half = 0.5 * (1.0 + th)
            a = (u * half).astype(BF)
            act[rows, fs] = a
            red = red + nn(a, wr[fs, :])
            slope = half + 0.5 * u * (1.0 - th * th) * (c0 * (1.0 + 3.0 * c1 * sq))
            g = (da * slope).astype(BF)
            dexp[rows, fs] = g
            ebg[:, fs] += fold8(g.astype(F32), jnp.sum)
        out[rows, :] = (mid + (red + rbias)).astype(BF)
        rsum[...] += fold8(dy.astype(F32), jnp.sum)
        return carry

    lax.fori_loop(0, T // 256, block, 0)

    def reduce_grad(f, carry):
        grad[rows_at(f, 256), :] = nn(act[:, rows_at(f, 256)].T, cot[...]).astype(BF)
        return carry

    lax.fori_loop(0, FF // 256, reduce_grad, 0)
    for r in range(NB):
        i = dst[r]
        ref = keeps if r < NB // 2 else sends
        for q in range(4):
            ref[r % (NB // 2), :, FF + 512 * q : FF + 512 * (q + 1)] = grad[rows_at(4 * i + q, 16), :]
    for f in range(4):
        grad[512 * f : 512 * (f + 1), :] = nn(n2_t[...], dexp[:, 512 * f : 512 * (f + 1)]).astype(BF)
    for r in range(NB):
        i = dst[r]
        ref = keeps if r < NB // 2 else sends
        for f in range(4):
            ref[r % (NB // 2), :, 512 * f : 512 * (f + 1)] = grad[rows_at(32 * f + i, 16), :]


def middle_kernel(n_parts, dst, cot, middle, dexp, wo, we, sp_t, gate_t, rt, vec, *refs):
    (mgrad, gm_t, delta, dl_t, sends, keeps, vsum, low, sg, grad, mix_t) = refs[n_parts:]
    join(refs[:n_parts], mix_t)
    gain = vec[VG + 2 : VG + 3, :]
    vsum[...] = jnp.zeros_like(vsum)
    dl_t[...] = jnp.zeros_like(dl_t)

    def block(b, carry):
        rows = rows_at(b, 256)
        h = nt(dexp[rows, :], we[...])
        mid = middle[rows, :]
        center = mid - jnp.mean(mid, axis=-1, keepdims=True)
        var = jnp.mean(center * center, axis=-1, keepdims=True)
        r = lax.rsqrt(var + 1e-05)
        n = center * r
        vsum[0:8, :] += fold8(h * n, jnp.sum)
        vsum[8:16, :] += fold8(h, jnp.sum)
        k = h * gain
        inner = r * (
            k - jnp.mean(k, axis=-1, keepdims=True) - n * jnp.mean(k * n, axis=-1, keepdims=True)
        )
        mg = cot[rows, :].astype(F32) + inner
        mgrad[rows, :] = mg
        ag = mg.astype(BF)
        low[rows, :] = ag
        sg[...] = nt(wo[...], ag)
        for h2 in range(2):
            cols = rows_at(2 * b + h2, 128)
            lane = slice(128 * h2, 128 * h2 + 128)
            routes = rt[:, cols]
            gate = gate_t[:, cols]
            gg = [0.0] * TOPK
            dd = [0.0] * TOPK

            def store(j, half, acc, cols=cols, gate=gate, gg=gg, dd=dd):
                at = 64 * j + 32 * half
                m = (acc * gate[j : j + 1, :]).astype(BF)
                gm_t[at : at + 32, cols] = m
                mixed = mix_t[at : at + 32, cols]
                gg[j] = gg[j] + jnp.sum(mixed * acc, axis=0, keepdims=True)
                dd[j] = dd[j] + jnp.sum(mixed * m.astype(F32), axis=0, keepdims=True)

            select_slots(lambda row, lane=lane: sg[row : row + 32, lane], routes, 128, store)
            gg = jnp.concatenate(gg, axis=0)
            delta[:, cols] = jnp.concatenate(dd, axis=0)
            lg = gate * (gg - jnp.sum(gate * gg, axis=0, keepdims=True))
            ids = lax.broadcasted_iota(jnp.int32, (E, 128), 0)
            dl = jnp.zeros((E, 128), F32)
            for j in range(TOPK):
                hit = ids == jnp.broadcast_to(routes[j : j + 1, :], (E, 128))
                dl = jnp.where(hit, jnp.broadcast_to(lg[j : j + 1, :], (E, 128)), dl)
            dl_t[:32, cols] = jnp.concatenate([dl, jnp.zeros((8, 128), F32)], axis=0).astype(BF)
        return carry

    lax.fori_loop(0, T // 256, block, 0)

    def output_grad(f, carry):
        grad[rows_at(f, 256), :] = nn(sp_t[rows_at(f, 256), :], low[...]).astype(BF)
        return carry

    lax.fori_loop(0, QW // 256, output_grad, 0)
    for r in range(NB):
        i = dst[r]
        ref = keeps if r < NB // 2 else sends
        for q in range(3):
            ref[r % (NB // 2), :, 512 * q : 512 * (q + 1)] = grad[rows_at(3 * i + q, 16), :]


def attend_back_kernel(lo, hi, first, n_parts, q_t, gm_t, ka, va, kv_t, delta, rt, *refs):
    dq_out, dkv_out, q_s, g_s, dq_s, lse = refs[-6:]
    join(refs[:n_parts], lse)
    row = lax.broadcasted_iota(jnp.int32, (64, 1024), 0)
    dkv_out[...] = jnp.zeros((T, 128), F32) if first else refs[n_parts][...]

    def block(b, carry):
        cols = rows_at(b, 128)
        for j in range(TOPK):
            lane = slice(128 * j, 128 * (j + 1))
            q_s[:64, lane] = q_t[64 * j : 64 * (j + 1), cols]
            g_s[:64, lane] = gm_t[64 * j : 64 * (j + 1), cols]
            rows = row[:, :128]
            tail = jnp.where(rows == 0, 1.0, 0.0)
            for k, term in enumerate(split_terms(-lse[j : j + 1, cols], 3)):
                tail = jnp.where(rows == k + 1, jnp.broadcast_to(term, (64, 128)), tail)
            q_s[64:, lane] = tail.astype(BF)
            tail = jnp.zeros((64, 128), F32)
            for k, term in enumerate(split_terms(-delta[j : j + 1, cols], 2)):
                tail = jnp.where(rows == k, jnp.broadcast_to(term, (64, 128)), tail)
            g_s[64:, lane] = tail.astype(BF)
        dq_s[...] = jnp.zeros_like(dq_s)
        full = b // 2

        def chunk(c, diagonal):
            at = rows_at(c, 256)
            e = jnp.exp2(nn(ka[at, :], q_s[...]) * SCALE2)
            if diagonal:
                at_s = lax.broadcasted_iota(jnp.int32, (256, 1024), 0) + c * 256
                at_t = (lax.broadcasted_iota(jnp.int32, (256, 1024), 1) & 127) + b * 128
                e = jnp.where(at_s <= at_t, e, 0.0)
            ds = (e * nn(va[at, :], g_s[...])).astype(BF)
            dq_s[...] += nn(kv_t[:64, at], ds)
            dkv_out[at, :64] += nt(ds, q_s[:64, :])
            dkv_out[at, 64:] += nt(e.astype(BF), g_s[:64, :])

        def step(c, carry):
            chunk(c, False)
            return carry

        lax.fori_loop(0, full, step, 0)
        chunk(full, True)

        def vals(j, half):
            return dq_s[32 * half : 32 * half + 32, 128 * j : 128 * (j + 1)] * HD**-0.5

        out_cols = rows_at(b - lo, 128)

        def store(e, half, block):
            at = 64 * e + 32 * half
            dq_out[at : at + 32, out_cols] = block

        spread_slots(vals, rt[:, cols], 128, store)
        return carry

    lax.fori_loop(lo, hi, block, 0)


def query_grad_kernel(n_parts, dst, dkv, dl_t, normed_t, w1, vsum, rsum, ebg, stat, *refs):
    parts = refs[:n_parts]
    dy_t, sends, keeps, grad, vecs, ysum, eb = refs[n_parts:]
    join(parts, dy_t.at[:QW])
    lane = lax.broadcasted_iota(jnp.int32, (T, 128), 1)
    kv = (dkv[...] * jnp.where(lane < 64, HD**-0.5, 1.0)).astype(BF)
    dy_t[QW:MISC, :] = kv.T
    dy_t[MISC:, :] = dl_t[...]
    cross = jnp.zeros((D, 1), F32)
    for c in range(C1 // 256):
        cs = slice(256 * c, 256 * (c + 1))
        g = nt(normed_t[...], dy_t[cs, :])
        grad[:, cs] = g
        cross = cross + jnp.sum(w1[:, cs].astype(F32) * g, axis=1, keepdims=True)
        total = dy_t[cs, 0:128].astype(F32)
        for k in range(1, T // 128):
            total = total + dy_t[cs, 128 * k : 128 * (k + 1)].astype(F32)
        ysum[cs, :] = total.astype(BF)
    vecs[...] = jnp.zeros_like(vecs)
    total = lambda x: jnp.sum(x, axis=0, keepdims=True)
    vecs[VG + 2 : VG + 3, :] = total(vsum[0:8, :])
    vecs[VG + 3 : VG + 4, :] = total(vsum[8:16, :])
    vecs[VG + 4 : VG + 5, :] = total(rsum[...])
    eb[...] = jnp.broadcast_to(total(ebg[...]), (128, FF)).T
    lanes = lax.broadcasted_iota(jnp.int32, (D, 128), 1)
    bias_grad = jnp.sum(nn(w1[...], ysum[...]), axis=1, keepdims=True)
    tail = w1[:, MISC:].astype(F32)
    gain = jnp.sum(jnp.where(lanes == VG, tail, 0.0), axis=1, keepdims=True)
    bias = jnp.sum(jnp.where(lanes == VG + 1, tail, 0.0), axis=1, keepdims=True)
    gain_grad = (cross - bias * bias_grad) / gain
    grad[:, MISC:] += (
        vecs[...].T + jnp.where(lanes == VG, gain_grad, 0.0) + jnp.where(lanes == VG + 1, bias_grad, 0.0)
    )
    for r in range(NB):
        i = dst[r]
        ref = keeps if r < NB // 2 else sends
        ref[r % (NB // 2), :, :MISC] = grad[rows_at(i, 16), :MISC].astype(BF)
        tail = grad[rows_at(i, 16), MISC:] + stat[...]
        for c in range(4):
            tail = tail + jnp.where(lanes[:16] == VG + 5 + c, eb[rows_at(4 * i + c, 16), :], 0.0)
        ref[r % (NB // 2), :, MISC:] = tail.astype(BF)


def input_grad_kernel(w1, dy_t, tok, mgrad, vec, out):
    gain = vec[VG : VG + 1, :]

    def block(b, carry):
        rows = rows_at(b, 256)
        h = nn(w1[...], dy_t[:, rows]).T
        x = tok[rows, :].astype(F32)
        center = x - jnp.mean(x, axis=-1, keepdims=True)
        var = jnp.mean(center * center, axis=-1, keepdims=True)
        r = lax.rsqrt(var + 1e-05)
        n = center * r
        k = h * gain
        inner = r * (
            k - jnp.mean(k, axis=-1, keepdims=True) - n * jnp.mean(k * n, axis=-1, keepdims=True)
        )
        out[rows, :] = (mgrad[rows, :] + inner).astype(BF)
        return carry

    lax.fori_loop(0, T // 256, block, 0)


SMEM = pltpu.SMEM
VMEM = pltpu.VMEM


def call(kernel, smem, args, outs, scratch=(), flops=0, after=(), smem_outs=0):
    specs = [pl.BlockSpec(memory_space=SMEM)] * smem
    specs += [pl.BlockSpec(memory_space=VMEM)] * (len(args) - smem)
    specs += [pl.BlockSpec(memory_space=pl.ANY)] * len(after)
    n_args = len(args)
    total = sum(math.prod(a.shape) * a.dtype.itemsize for a in args)
    total += sum(math.prod(s) * jnp.dtype(d).itemsize for s, d in outs)
    return pl.pallas_call(
        lambda *refs: kernel(*refs[:n_args], *refs[n_args + len(after) :]),
        out_shape=[jax.ShapeDtypeStruct(s, d) for s, d in outs],
        in_specs=specs,
        out_specs=[pl.BlockSpec(memory_space=VMEM)] * (len(outs) - smem_outs)
        + [pl.BlockSpec(memory_space=SMEM)] * smem_outs,
        scratch_shapes=[VMEM(s, d) for s, d in scratch],
        compiler_params=pltpu.CompilerParams(vmem_limit_bytes=60 * 1024 * 1024),
        cost_estimate=pl.CostEstimate(flops=flops, bytes_accessed=total, transcendentals=0),
    )(*args, *after)


def project(dst, length, tok, rt, pieces, after):
    return call(
        functools.partial(project_kernel, len(pieces)),
        2,
        (dst, length, tok, rt, *pieces),
        [
            ((D, C1), BF), ((D, T), BF), ((TOPK * HD, T), BF), ((128, T), BF), ((T, 128), BF), ((T, 128), BF),
            ((TOPK, T), F32), ((128, D), F32), ((16, 128), F32), ((8, FF), F32),
        ],
        [((C1, D), BF), ((C1, 256), F32), ((E, 128), F32), ((E, 128), F32), ((FF, 128), F32)],
        flops=2 * T * D * C1,
        after=after,
    )


def attend(lo, hi, q_t, ka, kv_t, gate_t, rt, after):
    n = 128 * (hi - lo)
    return call(
        functools.partial(attend_kernel, lo, hi),
        0,
        (q_t, ka, kv_t, gate_t, rt),
        [((TOPK * HD, n), F32), ((TOPK, n), F32), ((QW, n), BF)],
        [((128, 1024), BF), ((T, 1024), F32), ((64, 1024), F32)],
        flops=8 * TOPK * T * T * HD,
        after=after,
    )


def ffn(dst, tok, cot, vec, ebias, pieces, parts):
    half = NB // 2
    return call(
        functools.partial(ffn_kernel, len(pieces), len(parts)),
        1,
        (dst, tok, cot, vec, ebias, *pieces, *parts),
        [
            ((T, D), BF), ((T, D), F32), ((T, FF), BF), ((QW, D), BF), ((D, FF), BF), ((QW, T), BF),
            ((half, 16, 2 * FF), BF), ((half, 16, 2 * FF), BF), ((8, D), F32), ((8, FF), F32),
        ],
        [((FF, D), BF), ((T, FF), BF), ((D, T), BF), ((FF, D), BF)],
        flops=2 * T * D * (5 * FF + QW),
    )


def middle_back(dst, cot, middle, dexp, wo, we, sp_t, gate_t, rt, vec, mixed):
    half = NB // 2
    return call(
        functools.partial(middle_kernel, len(mixed)),
        1,
        (dst, cot, middle, dexp, wo, we, sp_t, gate_t, rt, vec, *mixed),
        [
            ((T, D), F32), ((TOPK * HD, T), BF), ((TOPK, T), F32), ((128, T), BF),
            ((half, 16, QW), BF), ((half, 16, QW), BF), ((16, D), F32),
        ],
        [((T, D), BF), ((QW, 256), F32), ((QW, D), BF), ((TOPK * HD, T), F32)],
        flops=2 * T * D * (FF + 2 * QW),
    )


def attend_back(lo, hi, q_t, gm_t, ka, va, kv_t, delta, rt, lse, dkv, after):
    return call(
        functools.partial(attend_back_kernel, lo, hi, dkv is None, len(lse)),
        0,
        (q_t, gm_t, ka, va, kv_t, delta, rt, *lse) + (() if dkv is None else (dkv,)),
        [((QW, 128 * (hi - lo)), BF), ((T, 128), F32)],
        [((128, 1024), BF), ((128, 1024), BF), ((64, 1024), F32), ((TOPK, T), F32)],
        flops=8 * TOPK * T * T * HD,
        after=after,
    )


def query_grads(dst, dkv, dl_t, normed_t, w1, vsum, rsum, ebg, stat, parts, after):
    half = NB // 2
    return call(
        functools.partial(query_grad_kernel, len(parts)),
        1,
        (dst, dkv, dl_t, normed_t, w1, vsum, rsum, ebg, stat, *parts),
        [((C1, T), BF), ((half, 16, C1), BF), ((half, 16, C1), BF)],
        [((D, C1), F32), ((128, D), F32), ((C1, 128), BF), ((FF, 128), F32)],
        flops=2 * T * D * C1,
        after=after,
    )


def input_grad(w1, dy_t, tok, mgrad, vec, after):
    return call(
        input_grad_kernel,
        0,
        (w1, dy_t, tok, mgrad, vec),
        [((T, D), BF)],
        flops=2 * T * D * C1,
        after=after,
    )[0]


def finish_ffn_kernel(keep, recv, expand, reduce):
    total = keep[0].astype(F32) + recv[0].astype(F32)
    expand[...] = total[:, :FF]
    for q in range(4):
        reduce[16 * q : 16 * (q + 1), :] = total[:, FF + 512 * q : FF + 512 * (q + 1)]


def finish_output_kernel(keep, recv, output):
    total = keep[0].astype(F32) + recv[0].astype(F32)
    for q in range(3):
        output[16 * q : 16 * (q + 1), :] = total[:, 512 * q : 512 * (q + 1)]


def finish_query_kernel(keep, recv, query, key_value, router, stats, fg, fb, sg, sb, rb, eb):
    total = keep[0].astype(F32) + recv[0].astype(F32)
    query[...] = total[:, :QW]
    key_value[...] = total[:, QW:MISC]
    router[...] = total[:, MISC : MISC + E]
    tail = jnp.concatenate([total[:, MISC:], jnp.zeros((112, 128), F32)], axis=0).T
    for k, ref in enumerate((fg, fb, sg, sb, rb)):
        ref[...] = tail[VG + k : VG + k + 1, :16]
    for c in range(4):
        eb[:, 16 * c : 16 * (c + 1)] = tail[VG + 5 + c : VG + 6 + c, :16]
    stats[...] = statistics(tail[ST : ST + 24, :])


def statistics(digits):
    counts, probs = jnp.zeros((1, 128), F32), jnp.zeros((1, 128), F32)
    for k in range(10):
        row = digits[k : k + 1, :] + pltpu.roll(digits[k + 10 : k + 11, :], 16, axis=1)
        if k < 4:
            counts = counts + row * 8.0**k
        else:
            probs = probs + row * 8.0 ** (k - 4)
    valid_total = jnp.sum(counts, axis=1, keepdims=True) / TOPK
    counts = E * counts / (TOPK * valid_total)
    probs = E * (probs / 128.0) / valid_total
    return jnp.concatenate([counts[:, :E], probs[:, :E]], axis=0)


def statistics_kernel(digits, stats):
    stats[...] = statistics(digits[...])


def finish(kernel, pair, outs):
    return call(kernel, 0, pair, [(s, F32) for s in outs])


MASKS = ((2, 4, 8, 16), (4, 2, 16, 8))
CORE = 1


def far(core, r):
    return sum(m for k, m in enumerate(MASKS[core]) if r >> k & 1)


def swap(x, step):
    perm = [(i, i ^ (CORE if step == 4 else MASKS[i & 1][step])) for i in range(32)]
    return lax.ppermute(x, AXES, perm)


def widen(held, step):
    return jnp.concatenate([held, swap(held, step)], axis=0)


def tie(x, *others):
    return lax.optimization_barrier((x, *others))[0]


def add(a, b):
    return (a.astype(F32) + b.astype(F32)).astype(BF)


def narrow(keep, recv):
    half = keep.shape[0] // 2
    send = add(keep[half:], recv[half:])
    return add(keep[:half], recv[:half]), send


def pack_kernel(
    paired, qw, kvw, rw, ow, ew, rw2, routes, fg, fb, sg, sb, rb, eb, one, two, rt, table, cols
):
    me = lax.axis_index(AXES)
    core = me & 1
    for r in range(16):
        if paired:
            near = jnp.where(core == 0, far(0, r), far(1, r))
            across = jnp.where(core == 0, far(1, r), far(0, r))
            table[r] = me ^ near
            table[16 + r] = me ^ CORE ^ across
        else:
            table[r] = r
            table[16 + r] = 16 + r
    rt[...] = routes[...].T
    if not paired:
        return
    cols[...] = jnp.zeros_like(cols)
    for k, ref in enumerate((fg, fb, sg, sb, rb)):
        cols[VG + k : VG + k + 1, :16] = ref[...].astype(F32)
    for c in range(4):
        cols[VG + 5 + c : VG + 6 + c, :16] = eb[:, 16 * c : 16 * (c + 1)].astype(F32)
    cols[:E, :16] = rw[...].astype(F32).T
    one[0, :, :QW] = qw[...]
    one[0, :, QW:MISC] = kvw[...]
    one[0, :, MISC:] = cols[...].T[:16, :].astype(BF)
    for q in range(3):
        two[0, :, 512 * q : 512 * (q + 1)] = ow[16 * q : 16 * (q + 1), :]
    two[0, :, 1536 : 1536 + FF] = ew[...]
    for q in range(4):
        two[0, :, 1536 + FF + 512 * q : 1536 + FF + 512 * (q + 1)] = rw2[16 * q : 16 * (q + 1), :]


def per_device(
    n_devices, tokens, lengths, routes, query_weight, key_value_weight, router_weight, output_weight,
    expand_weight, expand_bias, reduce_weight, reduce_bias, first_gain, first_bias, second_gain,
    second_bias, cotangent,
):
    paired = n_devices == NB
    tok, cot = tokens[0], cotangent[0]
    vectors = [first_gain, first_bias, second_gain, second_bias, reduce_bias, expand_bias]
    one, two, rt, table = call(
        functools.partial(pack_kernel, paired),
        0,
        (
            query_weight, key_value_weight, router_weight, output_weight, expand_weight, reduce_weight,
            routes[0], *[v.reshape(1, -1) for v in vectors],
        ),
        [((1, 16, C1), BF), ((1, 16, C2), BF), ((TOPK, T), jnp.int32), ((NB,), jnp.int32)],
        [((128, 128), F32)],
        smem_outs=1,
    )
    if paired:
        one = widen(widen(one, 0), 1)
        two = tie(two, one)
        one = widen(one, 2)
        two = tie(widen(two, 0), one)
        one = widen(one, 3)
        two = tie(widen(two, 1), one)
        pieces_one = [one, swap(one, 4)]
        after, coming = [two], swap(two, 2)
    else:
        gather = lambda w: lax.all_gather(w, AXES, axis=0, tiled=True)
        blocks = lambda w: w.reshape(NB, -1, 16, 512).transpose(0, 2, 1, 3).reshape(NB, 16, -1)
        columns = jnp.stack(vectors[:5], axis=1)
        fill = jnp.zeros((columns.shape[0], 128 - E - 5), BF)
        first = jnp.concatenate([query_weight, key_value_weight, router_weight, columns, fill], axis=1)
        pieces_one = [gather(first).reshape(NB, 16, C1)]
        parts = [blocks(gather(output_weight)), gather(expand_weight).reshape(NB, 16, FF)]
        pieces_two = [jnp.concatenate(parts + [blocks(gather(reduce_weight))], axis=2)]
        after = []

    w1, normed_t, q_t, kv_t, ka, va, gate_t, vec, stat, ebias = project(
        table, lengths, tok, rt, pieces_one, after
    )
    if not paired:
        ebias = jnp.broadcast_to(gather(expand_bias).astype(F32), (8, FF))
    mixed, lse, spread = [], [], []
    done = stat
    for step, (lo, hi) in zip((3, 4), ((0, 6), (6, 8))):
        if paired:
            two = jnp.concatenate([two, tie(coming, done)], axis=0)
            after, coming = [two], swap(two, step)
        m, top, sp = attend(lo, hi, q_t, ka, kv_t, gate_t, rt, after)
        mixed.append(m)
        lse.append(top)
        spread.append(sp)
        done = top
    if paired:
        pieces_two = [two, tie(coming, done)]
    out, middle, dexp, wo, we, sp_t, sends, keeps, rsum, ebg = ffn(
        table, tok, cot, vec, ebias, pieces_two, spread
    )
    ffn_sum = (keeps, sends)
    mgrad, gm_t, delta, dl_t, sends, keeps, vsum = middle_back(
        table, cot, middle, dexp, wo, we, sp_t, gate_t, rt, vec, mixed
    )
    output_sum = (keeps, sends)
    dkv, parts = None, []
    if paired:
        after = ffn_sum = narrow(ffn_sum[0], tie(swap(ffn_sum[1], 4), delta))
        steps = ((3, 4), (2, 3), (1, 2))
    else:
        after, steps = (), (None,) * 3
    for (lo, hi), step in zip(((0, 4), (4, 6), (6, 8)), steps):
        dq, dkv = attend_back(lo, hi, q_t, gm_t, ka, va, kv_t, delta, rt, lse, dkv, after)
        parts.append(dq)
        if paired:
            ffn_sum = narrow(ffn_sum[0], tie(swap(ffn_sum[1], step[0]), dkv))
            output_sum = narrow(output_sum[0], tie(swap(output_sum[1], step[1]), dkv))
            after = (*ffn_sum, *output_sum)
    dy_t, sends, keeps = query_grads(
        table, dkv, dl_t, normed_t, w1, vsum, rsum, ebg, stat, parts, after
    )
    query_sum = (keeps, sends)
    if paired:
        ffn_sum = (ffn_sum[0], tie(swap(ffn_sum[1], 0), sends))
        output_sum = narrow(output_sum[0], tie(swap(output_sum[1], 1), sends))
        query_sum = narrow(keeps, swap(tie(sends, ffn_sum[1], *output_sum), 4))
        after = query_sum
    tokens_grad = input_grad(w1, dy_t, tok, mgrad, vec, after)

    if paired:
        output_sum = (output_sum[0], swap(output_sum[1], 0))
        query_sum = (query_sum[0], tie(swap(query_sum[1], 3), tokens_grad))
        for step in (2, 1, 0):
            keep, send = narrow(*query_sum)
            query_sum = (keep, swap(send, step))
        expand_grad, reduce_grad = finish(finish_ffn_kernel, ffn_sum, [(16, FF), (64, D)])
        (output_grad,) = finish(finish_output_kernel, output_sum, [(48, D)])
        query_grad, key_value_grad, router_grad, router_stats, *rest = finish(
            finish_query_kernel,
            query_sum,
            [(16, QW), (16, 128), (16, E), (2, E)] + [(1, 16)] * 5 + [(1, 64)],
        )
        fg, fb, sg, sb, rb, expand_bias_grad = [g.reshape(-1) for g in rest]
    else:
        whole = lambda pair: jnp.concatenate(pair, axis=0)
        scatter = lambda g: lax.psum_scatter(g, AXES, scatter_dimension=0, tiled=True)
        rows_of = lambda g, n: g.reshape(NB, 16, n, 512).transpose(0, 2, 1, 3).reshape(NB * 16 * n, 512)
        g = whole(ffn_sum).astype(F32)
        expand_grad = scatter(g[:, :, :FF].reshape(D, FF))
        reduce_grad = scatter(rows_of(g[:, :, FF:], 4))
        output_grad = scatter(rows_of(whole(output_sum).astype(F32), 3))
        g = whole(query_sum).astype(F32).reshape(D, C1)
        query_grad, key_value_grad = scatter(g[:, :QW]), scatter(g[:, QW:MISC])
        router_grad = scatter(g[:, MISC : MISC + E])
        fg, fb, sg, sb, rb = [scatter(g[:, MISC + VG + k]) for k in range(5)]
        expand_bias_grad = scatter(jnp.sum(ebg, axis=0))
        digits = jnp.pad(lax.psum(stat[:, ST : ST + 24], AXES).T, ((0, 0), (0, 112)))
        (router_stats,) = call(statistics_kernel, 0, (digits,), [((2, E), F32)])
    return (
        out[None], tokens_grad[None], query_grad, key_value_grad, router_grad, output_grad, expand_grad,
        expand_bias_grad, reduce_grad, rb, fg, fb, sg, sb, router_stats,
    )


def solution(mesh):
    both = lambda n: P(AXES, *([None] * (n - 1)))
    in_specs = tuple(both(n) for n in (3, 1, 3, 2, 2, 2, 2, 2, 1, 2, 1, 1, 1, 1, 1, 3))
    out_specs = tuple(both(n) for n in (3, 3, 2, 2, 2, 2, 2, 1, 2, 1, 1, 1, 1, 1)) + (P(),)
    return jax.shard_map(
        functools.partial(per_device, mesh.size),
        mesh=mesh,
        in_specs=in_specs,
        out_specs=out_specs,
        check_vma=False,
    )
```
